32 devices in a mesh: grp: 2 (over x), din: 16 (over z, y, core).
Axes of the slice: x: 2, y: 2, z: 4, core: 2. Of those that a mesh axis runs over, the one named last changes fastest.
Arguments:
- tokens: bfloat16 [256, 16384], P('grp', 'din'), parts along dimension 0, may hold values from -6 to 6
- norm_gain: bfloat16 [16384], P('din'), may hold values from 0.25 to 1.75
- gate_weight: bfloat16 [16384, 13312], P(None, 'din'), may hold values from -0.046875 to 0.046875
- up_weight: bfloat16 [16384, 13312], P(None, 'din'), may hold values from -0.046875 to 0.046875
- down_weight: bfloat16 [13312, 16384], P('din'), may hold values from -0.078125 to 0.078125
Outputs:
- block_out: bfloat16 [256, 16384], P('grp', 'din'), parts along dimension 0
The draws below stay inside these ranges and needn't reach their ends.
There are 2 independent parts, one for each index of `grp`. The reference program is written for one: setup_inputs(seed, part) draws one part's arguments, and reference() takes and returns one part's arrays. A program takes and returns all parts, laid end to end along the dimension named above; an argument that names none is the same for every part. Nothing has to cross between parts.
All inputs are finite; a program needn't handle non-finite values.
Results may differ from the reference program's by a relative error of at most 0.0066.
Values may be sent and summed in bfloat16 or wider, within the bound.
A program may use at most 256 MiB of HBM per device.

```python
import jax
import jax.numpy as jnp
from jax import lax

D = 16384
HID = 13312
ROWS = 128


def strengthened(entries, key, source, target, shards_of, factor):
    def block_of(dim):
        return (jnp.arange(entries.shape[dim]) // (entries.shape[dim] // shards_of)).reshape((-1,) + (1,) * (entries.ndim - 1 - dim))

    near = jax.random.permutation(key, shards_of)[block_of(target)]
    second = (block_of(target) + shards_of // 2) % shards_of
    return jnp.where((block_of(source) == near) | (block_of(source) == second), factor * entries, entries)


def steps_of(rng, extent, cuts, smallest, top_value):
    def one(dim, parts):
        heights = jax.random.uniform(jax.random.fold_in(jax.random.fold_in(rng, 6), dim), (parts,), jnp.float32, smallest / len(cuts), top_value / len(cuts))
        return jnp.repeat(jnp.exp(heights), extent[dim] // parts).reshape((-1,) + (1,) * (len(extent) - dim - 1))

    gain = one(*cuts[0])
    for cut in cuts[1:]:
        gain = gain * one(*cut)
    return gain


def noise(stream_key, shape, spread, bound, pieces=(), held_as=jnp.bfloat16):
    entries = spread * jax.random.normal(stream_key, shape, jnp.float32)
    if pieces:
        entries = entries * steps_of(stream_key, shape, pieces, -0.22, 0.18)
    return jnp.clip(entries, -bound, bound).astype(held_as)


def bell_draw_with(stream_key, shape, scale, most, cuts, heavy, held_as=jnp.bfloat16):
    values = scale * jax.random.normal(stream_key, shape, jnp.float32)
    if cuts:
        values = values * steps_of(stream_key, shape, cuts, -0.22, 0.18)
    return jnp.clip(strengthened(values, jax.random.fold_in(stream_key, 3), *heavy), -most, most).astype(held_as)


def setup_inputs(seed: int = 0, part: int = 0) -> dict:
    key_of = jax.random.split(jax.random.key(seed), 6)
    part_splits = jax.random.split(jax.random.fold_in(key_of[5], part), 6)
    return {
        "tokens": noise(part_splits[0], (ROWS, D), 1.0, 6.0, ((1, 16),)),
        "norm_gain": jnp.clip(1.0 + 0.15 * jax.random.normal(key_of[1], (D,), jnp.float32), 0.25, 1.75).astype(jnp.bfloat16),
        "gate_weight": noise(key_of[2], (D, HID), D ** -0.5, 0.046875, ((1, 16),)),
        "up_weight": noise(key_of[3], (D, HID), D ** -0.5, 0.046875, ((1, 16),)),
        "down_weight": bell_draw_with(key_of[4], (HID, D), HID ** -0.5, 0.078125, ((0, 16),), (0, 1, 16, 2.0)),
    }


def reference(tokens, norm_gain, gate_weight, up_weight, down_weight):
    values = tokens.astype(jnp.float32)
    inverse_rms = lax.rsqrt(lax.optimization_barrier(jnp.mean(values * values, axis=1, keepdims=True)) + 1e-05)
    normed = (values * norm_gain.astype(jnp.float32) * inverse_rms).astype(jnp.bfloat16)
    gate = jnp.dot(normed, gate_weight, preferred_element_type=jnp.float32)
    up = jnp.dot(normed, up_weight, preferred_element_type=jnp.float32)
    hidden = (jax.nn.silu(gate) * up).astype(jnp.bfloat16)
    return jnp.dot(hidden, down_weight, preferred_element_type=jnp.float32).astype(jnp.bfloat16)
```

```python
import functools

import jax
import jax.numpy as jnp
from jax import lax
from jax.experimental import pallas as pl
from jax.experimental.pallas import tpu as pltpu
from jax.sharding import PartitionSpec as P

NBUF = 4
TILE = 256
EPS = 1e-05


def gathered(tokens, norm_gain, gate_weight, up_weight, down_weight):
    whole, gain = (
        lax.all_gather(tokens, "din", axis=1, tiled=True),
        lax.all_gather(norm_gain, "din", axis=0, tiled=True),
    )
    values = whole.astype(jnp.float32)
    inverse_rms = lax.rsqrt(jnp.mean(values * values, axis=1, keepdims=True) + EPS)
    normed = (values * gain.astype(jnp.float32) * inverse_rms).astype(jnp.bfloat16)
    gate = jnp.dot(normed, gate_weight, preferred_element_type=jnp.float32)
    up = jnp.dot(normed, up_weight, preferred_element_type=jnp.float32)
    hidden = (jax.nn.silu(gate) * up).astype(jnp.bfloat16)
    partial_terms = jnp.dot(hidden, down_weight, preferred_element_type=jnp.float32)
    return lax.psum_scatter(partial_terms, "din", scatter_dimension=1, tiled=True).astype(
        jnp.bfloat16
    )


def ffn_kernel(
    n, x_ref, g_ref, wg_hbm, wu_hbm, wd_hbm, o_ref,
    xbuf, wg, wu, wd, acc_g, acc_u, normed, hid, inv, msg, own, sib_out, sib_in, ring_out, ring_in,
    msg_s, msg_r, ag_s, ag_r, xs_s, xs_r, xo_s, xo_r, w_sem, d_sem, rs_s, rs_r, sb_s, sb_r,
):
    chips = n // 2
    zs = chips // 2
    half = chips // 2
    rows, block = x_ref.shape
    hr = rows // 2
    width = wg_hbm.shape[1]
    features = n * block
    me = lax.axis_index("din")
    core = me % 2
    my_z, my_y = me // 4, (me // 2) % 2
    pos = my_z + my_y * (chips - 1 - 2 * my_z)

    def at(p, c):
        p = (p + 2 * chips) % chips
        y = p // zs
        z = p + y * (chips - 1 - 2 * p)
        return (z * 2 + y) * 2 + c

    other = 1 - core
    sibling = {"din": at(pos, other)}
    toward = ({"din": at(pos + 1, core)}, {"din": at(pos - 1, core)})
    sign = (-1, 1)

    def block_at(j, e):
        k = (j + 1) // 2
        ends = jnp.where(j == 0, 1, jnp.where(j == 2 * half - 1, 1, 0))
        shift = jnp.where(ends == 1, k, (2 * e - 1) * k)
        flip = jnp.where(ends == 1, e, (j + 1) % 2)
        return at(pos + shift, core + flip * (1 - 2 * core))

    def weight_copies(i):
        d = block_at(i // 2, i % 2)
        start = pl.multiple_of(d * block, block)
        b = i % NBUF
        return (
            pltpu.make_async_copy(wg_hbm.at[pl.ds(start, block)], wg.at[b], w_sem.at[0, b]),
            pltpu.make_async_copy(wu_hbm.at[pl.ds(start, block)], wu.at[b], w_sem.at[1, b]),
        )

    def dest_at(t):
        u = t + 2
        k = half - u // 4
        w = u % 4
        mine = jnp.where(k == half, w - 2, jnp.where(k == 0, w % 2, w // 2))
        side = jnp.where(k == half, 1, 1 - 2 * (w % 2))
        c = other + mine * (1 - 2 * other)
        return at(pos + side * k, c)

    def down_copy(t):
        start = pl.multiple_of(dest_at(t) * block, block)
        return pltpu.make_async_copy(wd_hbm.at[:, pl.ds(start, block)], wd.at[t], d_sem.at[t])

    for i in range(NBUF):
        for copy in weight_copies(i):
            copy.start()

    barrier = pltpu.get_barrier_semaphore()

    def greet(k, c):
        pl.semaphore_signal(barrier, inc=1, device_id={"din": (me + k) % n}, device_id_type=pl.DeviceIdType.MESH)
        return c

    lax.fori_loop(1, n, greet, 0)

    xbuf[me] = x_ref[...]
    values = x_ref[...].astype(jnp.float32)
    squares = jnp.sum(values * values, axis=1, keepdims=True)
    msg[me, :, :block] = g_ref[...].astype(jnp.float32)
    msg[me, :, block:] = jnp.transpose(jnp.broadcast_to(squares, (rows, 128)))[0:1, :]
    acc_g[...] = jnp.zeros_like(acc_g)
    acc_u[...] = jnp.zeros_like(acc_u)

    pl.semaphore_wait(barrier, n - 1)

    def msg_copy(k, slot):
        return pltpu.make_async_remote_copy(
            msg.at[slot], msg.at[slot], msg_s.at[k], msg_r.at[k],
            device_id={"din": (me + k) % n}, device_id_type=pl.DeviceIdType.MESH,
        )

    def gather_copy(way, k, h, slot):
        part = xbuf.at[slot, pl.ds(h * hr, hr)]
        return pltpu.make_async_remote_copy(
            part, part, ag_s.at[way, k, h], ag_r.at[way, k, h],
            device_id=toward[way], device_id_type=pl.DeviceIdType.MESH,
        )

    def across_copy(way, k, h, slot):
        part = xbuf.at[slot, pl.ds(h * hr, hr)]
        return pltpu.make_async_remote_copy(
            part, part, xs_s.at[way, k, h], xs_r.at[way, k, h],
            device_id=sibling, device_id_type=pl.DeviceIdType.MESH,
        )

    def own_across(slot):
        return pltpu.make_async_remote_copy(
            xbuf.at[slot], xbuf.at[slot], xo_s, xo_r,
            device_id=sibling, device_id_type=pl.DeviceIdType.MESH,
        )

    def tell(k, c):
        msg_copy(k, me).start()
        return c

    lax.fori_loop(1, n, tell, 0)
    for h in (0, 1):
        for way in (0, 1):
            gather_copy(way, 1, h if way == 0 else 1 - h, me).start()
    own_across(me).start()

    def hear(k, c):
        msg_copy(k, (me - k + n) % n).wait_recv()
        return c

    lax.fori_loop(1, n, hear, 0)
    total = msg[0, :, block:]
    for i in range(1, n):
        total = total + msg[i, :, block:]
    scale = lax.rsqrt(total / features + EPS)
    inv[...] = jnp.transpose(jnp.broadcast_to(scale, (128, rows)))

    def pass_on(k, second):
        for way in (0, 1):
            h = way if not second else 1 - way
            slot = at(pos + sign[way] * k, core)
            gather_copy(way, k, h, slot).wait_recv()

            if second:
                @pl.when(k < half - 1)
                def _():
                    gather_copy(way, k + 1, h, slot).start()
            else:
                @pl.when(k < half)
                def _():
                    gather_copy(way, k + 1, h, slot).start()
            across_copy(way, k, h, slot).start()

    def across_wait(k, second):
        for way in (0, 1):
            h = way if not second else 1 - way
            across_copy(way, k, h, at(pos + sign[way] * k, other)).wait_recv()

    def gate_up(i, c):
        d = block_at(i // 2, i % 2)
        normed[...] = (
            xbuf[d].astype(jnp.float32) * msg[d, :, :block] * inv[:, 0:1]
        ).astype(jnp.bfloat16)
        for copy in weight_copies(i):
            copy.wait()
        b = i % NBUF
        for lo in range(0, width, TILE):
            cols = slice(lo, min(lo + TILE, width))
            acc_g[:, cols] += jnp.dot(normed[...], wg[b, :, cols], preferred_element_type=jnp.float32)
            acc_u[:, cols] += jnp.dot(normed[...], wu[b, :, cols], preferred_element_type=jnp.float32)

        @pl.when(i + NBUF < n)
        def _():
            for copy in weight_copies(i + NBUF):
                copy.start()

        @pl.when(i >= n // 2)
        def _():
            down_copy(2 * (i - n // 2)).start()
            down_copy(2 * (i - n // 2) + 1).start()

        return c

    def pair(j, c):
        @pl.when(j == 0)
        def _():
            own_across(at(pos, other)).wait_recv()

        k = (j + 1) // 2

        @pl.when(j == 1)
        def _():
            pass_on(1, False)

        @pl.when(jnp.logical_and(j % 2 == 1, j < 2 * half - 1))
        def _():
            pass_on(k, True)

        @pl.when(jnp.logical_and(j % 2 == 0, j > 0))
        def _():
            pass_on(k + 1, False)
            across_wait(k, False)
            across_wait(k, True)

        @pl.when(j == 2 * half - 1)
        def _():
            across_wait(half, False)

        return lax.fori_loop(2 * j, 2 * j + 2, gate_up, c)

    lax.fori_loop(0, n // 2, pair, 0)

    for lo in range(0, width, TILE):
        cols = slice(lo, min(lo + TILE, width))
        gate = acc_g[:, cols]
        hid[:, cols] = (gate / (1.0 + jnp.exp(-gate)) * acc_u[:, cols]).astype(jnp.bfloat16)

    def down_tiles(t):
        for lo in range(0, block, TILE):
            cols = slice(lo, lo + TILE)
            yield cols, jnp.dot(hid[...], wd[t, :, cols], preferred_element_type=jnp.float32)

    def sib_copy(p):
        return pltpu.make_async_remote_copy(
            sib_out.at[p], sib_in.at[p], sb_s.at[p], sb_r.at[p],
            device_id=sibling, device_id_type=pl.DeviceIdType.MESH,
        )

    def ring_copy(way, k, h):
        return pltpu.make_async_remote_copy(
            ring_out.at[way, k, pl.ds(h * hr, hr)], ring_in.at[way, k, pl.ds(h * hr, hr)],
            rs_s.at[way, k, h], rs_r.at[way, k, h],
            device_id=toward[way], device_id_type=pl.DeviceIdType.MESH,
        )

    def to_sibling(t, p):
        down_copy(t).wait()
        for cols, tile in down_tiles(t):
            sib_out[p, :, cols] = tile.astype(jnp.bfloat16)
        sib_copy(p).start()

    def to_own(t, side):
        down_copy(t).wait()
        for cols, tile in down_tiles(t):
            own[side, :, cols] = tile

    def ring_send(way, k, h, p, side, chained):
        at_rows = pl.ds(h * hr, hr)
        value = own[side, at_rows, :] + sib_in[p, at_rows, :].astype(jnp.float32)
        if chained:
            ring_copy(way, k + 1, h).wait_recv()
            value = value + ring_in[way, k + 1, at_rows, :].astype(jnp.float32)
        ring_out[way, k, at_rows, :] = value.astype(jnp.bfloat16)
        ring_copy(way, k, h).start()

    to_sibling(0, 0)
    to_own(1, 0)
    sib_copy(0).wait_recv()
    ring_send(0, half, 0, 0, 0, False)
    ring_send(1, half, 1, 0, 0, False)

    def distance(it, c):
        k = half - 1 - it
        t = 2 + 4 * it

        def give(side, c):
            to_sibling(t + side, 1 + 2 * it + side)
            return c

        def keep(side, c):
            to_own(t + 2 + side, side)
            return c

        lax.fori_loop(0, 2, give, 0)
        lax.fori_loop(0, 2, keep, 0)
        for side in (0, 1):
            sib_copy(1 + 2 * it + side).wait_recv()
        for way in (0, 1):
            h = 1 - way

            @pl.when(k == half - 1)
            def _():
                ring_send(way, k, h, 1 + 2 * it + way, way, False)

            @pl.when(k < half - 1)
            def _():
                ring_send(way, k, h, 1 + 2 * it + way, way, True)

        for way in (0, 1):
            ring_send(way, k, way, 1 + 2 * it + way, way, True)
        return c

    lax.fori_loop(0, half - 1, distance, 0)
    last = 2 * half - 1
    to_sibling(n - 2, last)
    to_own(n - 1, 0)
    sib_copy(last).wait_recv()
    own[0] = own[0] + sib_in[last].astype(jnp.float32)
    for h_first in (1, 0):
        for way in (0, 1):
            h = h_first if way == 0 else 1 - h_first
            at_rows = pl.ds(h * hr, hr)
            ring_copy(way, 1, h).wait_recv()
            own[0, at_rows, :] = own[0, at_rows, :] + ring_in[way, 1, at_rows, :].astype(jnp.float32)
    o_ref[...] = own[0].astype(o_ref.dtype)

    def told(k, c):
        msg_copy(k, me).wait_send()
        return c

    lax.fori_loop(1, n, told, 0)
    own_across(me).wait_send()
    for way in (0, 1):
        for k in range(1, half + 1):
            for h in (0, 1):
                if k == half and h != way:
                    continue
                gather_copy(way, k, h, at(pos + sign[way] * (k - 1), core)).wait_send()
                across_copy(way, k, h, at(pos + sign[way] * k, core)).wait_send()
                ring_copy(way, k, h).wait_send()
    for p in range(2 * half):
        sib_copy(p).wait_send()


def ringed(n, tokens, norm_gain, gate_weight, up_weight, down_weight):
    rows, block = tokens.shape
    width = gate_weight.shape[1]
    half = n // 4
    bf16, f32 = jnp.bfloat16, jnp.float32
    dma = pltpu.SemaphoreType.DMA
    vmem = pl.BlockSpec(memory_space=pltpu.VMEM)
    hbm = pl.BlockSpec(memory_space=pl.ANY)
    return pl.pallas_call(
        functools.partial(ffn_kernel, n),
        out_shape=jax.ShapeDtypeStruct((rows, block), bf16),
        in_specs=[vmem, vmem, hbm, hbm, hbm],
        out_specs=vmem,
        scratch_shapes=[
            pltpu.VMEM((n, rows, block), bf16),
            pltpu.VMEM((NBUF, block, width), bf16),
            pltpu.VMEM((NBUF, block, width), bf16),
            pltpu.VMEM((n, width, block), bf16),
            pltpu.VMEM((rows, width), f32),
            pltpu.VMEM((rows, width), f32),
            pltpu.VMEM((rows, block), bf16),
            pltpu.VMEM((rows, width), bf16),
            pltpu.VMEM((rows, 128), f32),
            pltpu.VMEM((n, 1, block + 128), f32),
            pltpu.VMEM((2, rows, block), f32),
            pltpu.VMEM((2 * half, rows, block), bf16),
            pltpu.VMEM((2 * half, rows, block), bf16),
            pltpu.VMEM((2, half + 1, rows, block), bf16),
            pltpu.VMEM((2, half + 1, rows, block), bf16),
            dma((n,)), dma((n,)),
            dma((2, half + 1, 2)), dma((2, half + 1, 2)),
            dma((2, half + 1, 2)), dma((2, half + 1, 2)),
            dma, dma,
            dma((2, NBUF)), dma((n,)),
            dma((2, half + 1, 2)), dma((2, half + 1, 2)),
            dma((2 * half,)), dma((2 * half,)),
        ],
        compiler_params=pltpu.CompilerParams(
            collective_id=0, has_side_effects=True, vmem_limit_bytes=64 * 2**20 - 2**17
        ),
        cost_estimate=pl.CostEstimate(
            flops=6 * rows * n * block * width, bytes_accessed=6 * n * block * width, transcendentals=rows * width
        ),
        name="ffn_ring",
    )(tokens, norm_gain.reshape(1, block), gate_weight, up_weight, down_weight)


def solution(mesh):
    n = mesh.shape["din"]

    def local(tokens, norm_gain, gate_weight, up_weight, down_weight):
        args = (tokens, norm_gain, gate_weight, up_weight, down_weight)
        if n == 16 and tokens.shape[0] == 128 and tokens.shape[1] % TILE == 0 and gate_weight.shape[1] % 16 == 0:
            return ringed(n, *args)
        return gathered(*args)

    in_specs = (P("grp", "din"), P("din"), P(None, "din"), P(None, "din"), P("din", None))
    out_specs = P("grp", "din")
    return jax.shard_map(local, mesh=mesh, in_specs=in_specs, out_specs=out_specs, check_vma=False)
```

```python
import functools

import jax
import jax.numpy as jnp
from jax import lax
from jax.experimental import pallas as pl
from jax.experimental.pallas import tpu as pltpu
from jax.sharding import PartitionSpec as P

NBUF = 4
TILE = 256
EPS = 1e-05


def gathered(tokens, norm_gain, gate_weight, up_weight, down_weight):
    whole, gain = (
        lax.all_gather(tokens, "din", axis=1, tiled=True),
        lax.all_gather(norm_gain, "din", axis=0, tiled=True),
    )
    values = whole.astype(jnp.float32)
    inverse_rms = lax.rsqrt(jnp.mean(values * values, axis=1, keepdims=True) + EPS)
    normed = (values * gain.astype(jnp.float32) * inverse_rms).astype(jnp.bfloat16)
    gate = jnp.dot(normed, gate_weight, preferred_element_type=jnp.float32)
    up = jnp.dot(normed, up_weight, preferred_element_type=jnp.float32)
    hidden = (jax.nn.silu(gate) * up).astype(jnp.bfloat16)
    partial_terms = jnp.dot(hidden, down_weight, preferred_element_type=jnp.float32)
    return lax.psum_scatter(partial_terms, "din", scatter_dimension=1, tiled=True).astype(
        jnp.bfloat16
    )


def across_last(a, b):
    return lax.dot_general(a, b, (((1,), (1,)), ((), ())), preferred_element_type=jnp.float32)


def ffn_kernel(
    n, x_ref, g_ref, wg_hbm, wu_hbm, wd_hbm, o_ref,
    xbuf, wg, wu, wd, acc_g, acc_u, normed, hid, inv, msg, own, sib_out, sib_in, ring_out, ring_in,
    msg_s, msg_r, ag_s, ag_r, xs_s, xs_r, xo_s, xo_r, w_sem, d_sem, rs_s, rs_r, sb_s, sb_r,
):
    chips = n // 2
    zs = chips // 2
    half = chips // 2
    rows, block = x_ref.shape
    hr = rows // 2
    width = wg_hbm.shape[0]
    features = n * block
    me = lax.axis_index("din")
    core = me % 2
    my_z, my_y = me // 4, (me // 2) % 2
    pos = my_z + my_y * (chips - 1 - 2 * my_z)

    def at(p, c):
        p = (p + 2 * chips) % chips
        y = p // zs
        z = p + y * (chips - 1 - 2 * p)
        return (z * 2 + y) * 2 + c

    other = 1 - core
    sibling = {"din": at(pos, other)}
    toward = ({"din": at(pos + 1, core)}, {"din": at(pos - 1, core)})
    sign = (-1, 1)

    def block_at(j, e):
        k = (j + 1) // 2
        ends = jnp.where(j == 0, 1, jnp.where(j == 2 * half - 1, 1, 0))
        shift = jnp.where(ends == 1, k, (2 * e - 1) * k)
        flip = jnp.where(ends == 1, e, (j + 1) % 2)
        return at(pos + shift, core + flip * (1 - 2 * core))

    def weight_copies(i):
        d = block_at(i // 2, i % 2)
        start = pl.multiple_of(d * block, block)
        b = i % NBUF
        return (
            pltpu.make_async_copy(wg_hbm.at[:, pl.ds(start, block)], wg.at[b], w_sem.at[0, b]),
            pltpu.make_async_copy(wu_hbm.at[:, pl.ds(start, block)], wu.at[b], w_sem.at[1, b]),
        )

    def dest_at(t):
        u = t + 2
        k = half - u // 4
        w = u % 4
        mine = jnp.where(k == half, w - 2, jnp.where(k == 0, w % 2, w // 2))
        side = jnp.where(k == half, 1, 1 - 2 * (w % 2))
        c = other + mine * (1 - 2 * other)
        return at(pos + side * k, c)

    def down_copy(t):
        start = pl.multiple_of(dest_at(t) * block, block)
        return pltpu.make_async_copy(wd_hbm.at[:, pl.ds(start, block)], wd.at[t], d_sem.at[t])

    for i in range(NBUF):
        for copy in weight_copies(i):
            copy.start()

    barrier = pltpu.get_barrier_semaphore()

    def greet(k, c):
        pl.semaphore_signal(barrier, inc=1, device_id={"din": (me + k) % n}, device_id_type=pl.DeviceIdType.MESH)
        return c

    lax.fori_loop(1, n, greet, 0)

    xbuf[me] = x_ref[...]
    values = x_ref[...].astype(jnp.float32)
    squares = jnp.sum(values * values, axis=1, keepdims=True)
    msg[me, :, :block] = g_ref[...].astype(jnp.float32)
    msg[me, :, block:] = jnp.transpose(jnp.broadcast_to(squares, (rows, 128)))[0:1, :]
    acc_g[...] = jnp.zeros_like(acc_g)
    acc_u[...] = jnp.zeros_like(acc_u)

    pl.semaphore_wait(barrier, n - 1)

    def msg_copy(k, slot):
        return pltpu.make_async_remote_copy(
            msg.at[slot], msg.at[slot], msg_s.at[k], msg_r.at[k],
            device_id={"din": (me + k) % n}, device_id_type=pl.DeviceIdType.MESH,
        )

    def gather_copy(way, k, h, slot):
        part = xbuf.at[slot, pl.ds(h * hr, hr)]
        return pltpu.make_async_remote_copy(
            part, part, ag_s.at[way, k, h], ag_r.at[way, k, h],
            device_id=toward[way], device_id_type=pl.DeviceIdType.MESH,
        )

    def across_copy(way, k, h, slot):
        part = xbuf.at[slot, pl.ds(h * hr, hr)]
        return pltpu.make_async_remote_copy(
            part, part, xs_s.at[way, k, h], xs_r.at[way, k, h],
            device_id=sibling, device_id_type=pl.DeviceIdType.MESH,
        )

    def own_across(slot):
        return pltpu.make_async_remote_copy(
            xbuf.at[slot], xbuf.at[slot], xo_s, xo_r,
            device_id=sibling, device_id_type=pl.DeviceIdType.MESH,
        )

    def tell(k, c):
        msg_copy(k, me).start()
        return c

    lax.fori_loop(1, n, tell, 0)
    for h in (0, 1):
        for way in (0, 1):
            gather_copy(way, 1, h if way == 0 else 1 - h, me).start()
    own_across(me).start()

    def hear(k, c):
        msg_copy(k, (me - k + n) % n).wait_recv()
        return c

    lax.fori_loop(1, n, hear, 0)
    total = msg[0, :, block:]
    for i in range(1, n):
        total = total + msg[i, :, block:]
    scale = lax.rsqrt(total / features + EPS)
    inv[...] = jnp.transpose(jnp.broadcast_to(scale, (128, rows)))

    def pass_on(k, second):
        for way in (0, 1):
            h = way if not second else 1 - way
            slot = at(pos + sign[way] * k, core)
            gather_copy(way, k, h, slot).wait_recv()

            if second:
                @pl.when(k < half - 1)
                def _():
                    gather_copy(way, k + 1, h, slot).start()
            else:
                @pl.when(k < half)
                def _():
                    gather_copy(way, k + 1, h, slot).start()
            across_copy(way, k, h, slot).start()

    def across_wait(k, second):
        for way in (0, 1):
            h = way if not second else 1 - way
            across_copy(way, k, h, at(pos + sign[way] * k, other)).wait_recv()

    def gate_up(i, c):
        d = block_at(i // 2, i % 2)
        normed[...] = (
            xbuf[d].astype(jnp.float32) * msg[d, :, :block] * inv[:, 0:1]
        ).astype(jnp.bfloat16)
        for copy in weight_copies(i):
            copy.wait()
        b = i % NBUF
        for lo in range(0, width, TILE):
            cols = slice(lo, min(lo + TILE, width))
            acc_g[:, cols] += across_last(normed[...], wg[b, cols])
            acc_u[:, cols] += across_last(normed[...], wu[b, cols])

        @pl.when(i + NBUF < n)
        def _():
            for copy in weight_copies(i + NBUF):
                copy.start()

        @pl.when(i >= n // 2)
        def _():
            down_copy(2 * (i - n // 2)).start()
            down_copy(2 * (i - n // 2) + 1).start()

        return c

    def pair(j, c):
        @pl.when(j == 0)
        def _():
            own_across(at(pos, other)).wait_recv()

        k = (j + 1) // 2

        @pl.when(j == 1)
        def _():
            pass_on(1, False)

        @pl.when(jnp.logical_and(j % 2 == 1, j < 2 * half - 1))
        def _():
            pass_on(k, True)

        @pl.when(jnp.logical_and(j % 2 == 0, j > 0))
        def _():
            pass_on(k + 1, False)
            across_wait(k, False)
            across_wait(k, True)

        @pl.when(j == 2 * half - 1)
        def _():
            across_wait(half, False)

        return lax.fori_loop(2 * j, 2 * j + 2, gate_up, c)

    lax.fori_loop(0, n // 2, pair, 0)

    for lo in range(0, width, TILE):
        cols = slice(lo, min(lo + TILE, width))
        gate = acc_g[:, cols]
        hid[:, cols] = (gate / (1.0 + jnp.exp(-gate)) * acc_u[:, cols]).astype(jnp.bfloat16)

    def down_tiles(t):
        for lo in range(0, block, TILE):
            cols = slice(lo, lo + TILE)
            yield cols, jnp.dot(hid[...], wd[t, :, cols], preferred_element_type=jnp.float32)

    def sib_copy(p):
        return pltpu.make_async_remote_copy(
            sib_out.at[p], sib_in.at[p], sb_s.at[p], sb_r.at[p],
            device_id=sibling, device_id_type=pl.DeviceIdType.MESH,
        )

    def ring_copy(way, k, h):
        return pltpu.make_async_remote_copy(
            ring_out.at[way, k, pl.ds(h * hr, hr)], ring_in.at[way, k, pl.ds(h * hr, hr)],
            rs_s.at[way, k, h], rs_r.at[way, k, h],
            device_id=toward[way], device_id_type=pl.DeviceIdType.MESH,
        )

    def to_sibling(t, p):
        down_copy(t).wait()
        for cols, tile in down_tiles(t):
            sib_out[p, :, cols] = tile.astype(jnp.bfloat16)
        sib_copy(p).start()

    def to_own(t, side):
        down_copy(t).wait()
        for cols, tile in down_tiles(t):
            own[side, :, cols] = tile

    def ring_send(way, k, h, p, side, chained):
        at_rows = pl.ds(h * hr, hr)
        value = own[side, at_rows, :] + sib_in[p, at_rows, :].astype(jnp.float32)
        if chained:
            ring_copy(way, k + 1, h).wait_recv()
            value = value + ring_in[way, k + 1, at_rows, :].astype(jnp.float32)
        ring_out[way, k, at_rows, :] = value.astype(jnp.bfloat16)
        ring_copy(way, k, h).start()

    to_sibling(0, 0)
    to_own(1, 0)
    sib_copy(0).wait_recv()
    ring_send(0, half, 0, 0, 0, False)
    ring_send(1, half, 1, 0, 0, False)

    def distance(it, c):
        k = half - 1 - it
        t = 2 + 4 * it

        def give(side, c):
            to_sibling(t + side, 1 + 2 * it + side)
            return c

        def keep(side, c):
            to_own(t + 2 + side, side)
            return c

        lax.fori_loop(0, 2, give, 0)
        lax.fori_loop(0, 2, keep, 0)
        for side in (0, 1):
            sib_copy(1 + 2 * it + side).wait_recv()
        for way in (0, 1):
            h = 1 - way

            @pl.when(k == half - 1)
            def _():
                ring_send(way, k, h, 1 + 2 * it + way, way, False)

            @pl.when(k < half - 1)
            def _():
                ring_send(way, k, h, 1 + 2 * it + way, way, True)

        for way in (0, 1):
            ring_send(way, k, way, 1 + 2 * it + way, way, True)
        return c

    lax.fori_loop(0, half - 1, distance, 0)
    last = 2 * half - 1
    to_sibling(n - 2, last)
    to_own(n - 1, 0)
    sib_copy(last).wait_recv()
    own[0] = own[0] + sib_in[last].astype(jnp.float32)
    for h_first in (1, 0):
        for way in (0, 1):
            h = h_first if way == 0 else 1 - h_first
            at_rows = pl.ds(h * hr, hr)
            ring_copy(way, 1, h).wait_recv()
            own[0, at_rows, :] = own[0, at_rows, :] + ring_in[way, 1, at_rows, :].astype(jnp.float32)
    o_ref[...] = own[0].astype(o_ref.dtype)

    def told(k, c):
        msg_copy(k, me).wait_send()
        return c

    lax.fori_loop(1, n, told, 0)
    own_across(me).wait_send()
    for way in (0, 1):
        for k in range(1, half + 1):
            for h in (0, 1):
                if k == half and h != way:
                    continue
                gather_copy(way, k, h, at(pos + sign[way] * (k - 1), core)).wait_send()
                across_copy(way, k, h, at(pos + sign[way] * k, core)).wait_send()
                ring_copy(way, k, h).wait_send()
    for p in range(2 * half):
        sib_copy(p).wait_send()


def ringed(n, tokens, norm_gain, gate_weight, up_weight, down_weight):
    rows, block = tokens.shape
    width = gate_weight.shape[1]
    half = n // 4
    bf16, f32 = jnp.bfloat16, jnp.float32
    dma = pltpu.SemaphoreType.DMA
    vmem = pl.BlockSpec(memory_space=pltpu.VMEM)
    hbm = pl.BlockSpec(memory_space=pl.ANY)
    return pl.pallas_call(
        functools.partial(ffn_kernel, n),
        out_shape=jax.ShapeDtypeStruct((rows, block), bf16),
        in_specs=[vmem, vmem, hbm, hbm, hbm],
        out_specs=vmem,
        scratch_shapes=[
            pltpu.VMEM((n, rows, block), bf16),
            pltpu.VMEM((NBUF, width, block), bf16),
            pltpu.VMEM((NBUF, width, block), bf16),
            pltpu.VMEM((n, width, block), bf16),
            pltpu.VMEM((rows, width), f32),
            pltpu.VMEM((rows, width), f32),
            pltpu.VMEM((rows, block), bf16),
            pltpu.VMEM((rows, width), bf16),
            pltpu.VMEM((rows, 128), f32),
            pltpu.VMEM((n, 1, block + 128), f32),
            pltpu.VMEM((2, rows, block), f32),
            pltpu.VMEM((2 * half, rows, block), bf16),
            pltpu.VMEM((2 * half, rows, block), bf16),
            pltpu.VMEM((2, half + 1, rows, block), bf16),
            pltpu.VMEM((2, half + 1, rows, block), bf16),
            dma((n,)), dma((n,)),
            dma((2, half + 1, 2)), dma((2, half + 1, 2)),
            dma((2, half + 1, 2)), dma((2, half + 1, 2)),
            dma, dma,
            dma((2, NBUF)), dma((n,)),
            dma((2, half + 1, 2)), dma((2, half + 1, 2)),
            dma((2 * half,)), dma((2 * half,)),
        ],
        compiler_params=pltpu.CompilerParams(
            collective_id=0, has_side_effects=True, vmem_limit_bytes=64 * 2**20 - 2**17
        ),
        cost_estimate=pl.CostEstimate(
            flops=6 * rows * n * block * width, bytes_accessed=6 * n * block * width, transcendentals=rows * width
        ),
        name="ffn_ring",
    )(tokens, norm_gain.reshape(1, block), gate_weight.T, up_weight.T, down_weight)


def solution(mesh):
    n = mesh.shape["din"]

    def local(tokens, norm_gain, gate_weight, up_weight, down_weight):
        args = (tokens, norm_gain, gate_weight, up_weight, down_weight)
        if n == 16 and tokens.shape[0] == 128 and tokens.shape[1] % TILE == 0 and gate_weight.shape[1] % 16 == 0:
            return ringed(n, *args)
        return gathered(*args)

    in_specs = (P("grp", "din"), P("din"), P(None, "din"), P(None, "din"), P("din", None))
    out_specs = P("grp", "din")
    return jax.shard_map(local, mesh=mesh, in_specs=in_specs, out_specs=out_specs, check_vma=False)
```

```python
import functools

import jax
import jax.numpy as jnp
from jax import lax
from jax.experimental import pallas as pl
from jax.experimental.pallas import tpu as pltpu
from jax.sharding import PartitionSpec as P

NBUF = 4
EARLY = 4
TILE = 256
EPS = 1e-05


def gathered(tokens, norm_gain, gate_weight, up_weight, down_weight):
    whole, gain = (
        lax.all_gather(tokens, "din", axis=1, tiled=True),
        lax.all_gather(norm_gain, "din", axis=0, tiled=True),
    )
    values = whole.astype(jnp.float32)
    inverse_rms = lax.rsqrt(jnp.mean(values * values, axis=1, keepdims=True) + EPS)
    normed = (values * gain.astype(jnp.float32) * inverse_rms).astype(jnp.bfloat16)
    gate = jnp.dot(normed, gate_weight, preferred_element_type=jnp.float32)
    up = jnp.dot(normed, up_weight, preferred_element_type=jnp.float32)
    hidden = (jax.nn.silu(gate) * up).astype(jnp.bfloat16)
    partial_terms = jnp.dot(hidden, down_weight, preferred_element_type=jnp.float32)
    return lax.psum_scatter(partial_terms, "din", scatter_dimension=1, tiled=True).astype(
        jnp.bfloat16
    )


def across_last(a, b):
    return lax.dot_general(a, b, (((1,), (1,)), ((), ())), preferred_element_type=jnp.float32)


def ffn_kernel(
    n, x_ref, g_ref, wg_hbm, wu_hbm, wd_hbm, o_ref,
    xbuf, wg, wu, wd, acc_g, acc_u, normed, hid, inv, msg, own, sib_out, sib_in, ring_out, ring_in,
    msg_s, msg_r, ag_s, ag_r, xs_s, xs_r, xo_s, xo_r, w_sem, d_sem, rs_s, rs_r, sb_s, sb_r,
):
    chips = n // 2
    zs = chips // 2
    half = chips // 2
    rows, block = x_ref.shape
    hr = rows // 2
    hb = block // 2
    width = wg_hbm.shape[0]
    features = n * block
    me = lax.axis_index("din")
    core = me % 2
    my_z, my_y = me // 4, (me // 2) % 2
    pos = my_z + my_y * (chips - 1 - 2 * my_z)

    def at(p, c):
        p = (p + 2 * chips) % chips
        y = p // zs
        z = p + y * (chips - 1 - 2 * p)
        return (z * 2 + y) * 2 + c

    other = 1 - core
    sibling = {"din": at(pos, other)}
    toward = ({"din": at(pos + 1, core)}, {"din": at(pos - 1, core)})
    sign = (-1, 1)

    def piece_at(u, e):
        k = (u + 2) // 4
        second = ((u + 2) % 4) // 2
        slot = at(pos + (2 * e - 1) * k, core + (u % 2) * (1 - 2 * core))
        return slot, e + second * (1 - 2 * e)

    def weight_copies(u):
        b = u % NBUF
        copies = []
        for e in (0, 1):
            slot, h = piece_at(u, e)
            source = pl.ds(pl.multiple_of(slot * block + h * hb, hb), hb)
            for which, (whole, held) in enumerate(((wg_hbm, wg), (wu_hbm, wu))):
                copies.append(
                    pltpu.make_async_copy(
                        whole.at[:, source], held.at[b, :, pl.ds(e * hb, hb)], w_sem.at[which, e, b]
                    )
                )
        return copies

    def dest_at(t):
        u = t + 2
        k = half - u // 4
        w = u % 4
        mine = jnp.where(k == half, w - 2, jnp.where(k == 0, w % 2, w // 2))
        side = jnp.where(k == half, 1, 1 - 2 * (w % 2))
        c = other + mine * (1 - 2 * other)
        return at(pos + side * k, c)

    def down_copy(t):
        start = pl.multiple_of(dest_at(t) * block, block)
        return pltpu.make_async_copy(wd_hbm.at[:, pl.ds(start, block)], wd.at[t], d_sem.at[t])

    for i in range(NBUF):
        for copy in weight_copies(i):
            copy.start()
    for t in range(EARLY):
        down_copy(t).start()

    barrier = pltpu.get_barrier_semaphore()

    def greet(k, c):
        pl.semaphore_signal(barrier, inc=1, device_id={"din": (me + k) % n}, device_id_type=pl.DeviceIdType.MESH)
        return c

    lax.fori_loop(1, n, greet, 0)

    for h in (0, 1):
        xbuf[me, h] = x_ref[:, h * hb : (h + 1) * hb]
    values = x_ref[...].astype(jnp.float32)
    squares = jnp.sum(values * values, axis=1, keepdims=True)
    msg[me, :, :block] = g_ref[...].astype(jnp.float32).reshape(1, block)
    msg[me, :, block:] = jnp.transpose(jnp.broadcast_to(squares, (rows, 128)))[0:1, :]
    acc_g[...] = jnp.zeros_like(acc_g)
    acc_u[...] = jnp.zeros_like(acc_u)

    pl.semaphore_wait(barrier, n - 1)

    def msg_copy(k, slot):
        return pltpu.make_async_remote_copy(
            msg.at[slot], msg.at[slot], msg_s.at[k], msg_r.at[k],
            device_id={"din": (me + k) % n}, device_id_type=pl.DeviceIdType.MESH,
        )

    def gather_copy(way, k, h, slot):
        part = xbuf.at[slot, h]
        return pltpu.make_async_remote_copy(
            part, part, ag_s.at[way, k, h], ag_r.at[way, k, h],
            device_id=toward[way], device_id_type=pl.DeviceIdType.MESH,
        )

    def across_copy(way, k, h, slot):
        part = xbuf.at[slot, h]
        return pltpu.make_async_remote_copy(
            part, part, xs_s.at[way, k, h], xs_r.at[way, k, h],
            device_id=sibling, device_id_type=pl.DeviceIdType.MESH,
        )

    def own_across(slot):
        return pltpu.make_async_remote_copy(
            xbuf.at[slot], xbuf.at[slot], xo_s, xo_r,
            device_id=sibling, device_id_type=pl.DeviceIdType.MESH,
        )

    def tell(k, c):
        msg_copy(k, me).start()
        return c

    for way in (0, 1):
        gather_copy(way, 1, way, me).start()
    lax.fori_loop(1, n, tell, 0)
    for way in (0, 1):
        gather_copy(way, 1, 1 - way, me).start()
    own_across(me).start()

    def hear(k, c):
        msg_copy(k, (me - k + n) % n).wait_recv()
        return c

    lax.fori_loop(1, n, hear, 0)
    total = msg[0, :, block:]
    for i in range(1, n):
        total = total + msg[i, :, block:]
    scale = lax.rsqrt(total / features + EPS)
    inv[...] = jnp.transpose(jnp.broadcast_to(scale, (128, rows)))

    def pass_on(k, second):
        for way in (0, 1):
            h = way if not second else 1 - way
            slot = at(pos + sign[way] * k, core)
            gather_copy(way, k, h, slot).wait_recv()

            if second:
                @pl.when(k < half - 1)
                def _():
                    gather_copy(way, k + 1, h, slot).start()
            else:
                @pl.when(k < half)
                def _():
                    gather_copy(way, k + 1, h, slot).start()
            across_copy(way, k, h, slot).start()

    def across_wait(k, second):
        for way in (0, 1):
            h = way if not second else 1 - way
            across_copy(way, k, h, at(pos + sign[way] * k, other)).wait_recv()

    def unit(u, c):
        k = (u + 2) // 4
        second = ((u + 2) % 4) // 2
        mine = u % 2 == 0

        @pl.when(u == 1)
        def _():
            own_across(at(pos, other)).wait_recv()

        for turn in (0, 1):
            now = jnp.logical_and(u > 1, second == turn)

            @pl.when(jnp.logical_and(now, mine))
            def _():
                pass_on(k, turn == 1)

            @pl.when(jnp.logical_and(now, u % 2 == 1))
            def _():
                across_wait(k, turn == 1)

        for e in (0, 1):
            slot, h = piece_at(u, e)
            gain = msg[slot, :, pl.ds(pl.multiple_of(h * hb, hb), hb)]
            normed[:, e * hb : (e + 1) * hb] = (
                xbuf[slot, h].astype(jnp.float32) * gain * inv[:, 0:1]
            ).astype(jnp.bfloat16)
        for copy in weight_copies(u):
            copy.wait()
        b = u % NBUF
        acc_g[...] += across_last(wg[b], normed[...])
        acc_u[...] += across_last(wu[b], normed[...])

        @pl.when(u + NBUF < n)
        def _():
            for copy in weight_copies(u + NBUF):
                copy.start()

        @pl.when(u + EARLY < n)
        def _():
            down_copy(u + EARLY).start()

        return c

    lax.fori_loop(0, n, unit, 0)

    for lo in range(0, width, 128):
        part = slice(lo, min(lo + 128, width))
        gate = acc_g[part]
        hidden = gate / (1.0 + jnp.exp(-gate)) * acc_u[part]
        hid[:, part] = jnp.transpose(hidden).astype(jnp.bfloat16)

    def down_tiles(t):
        for lo in range(0, block, TILE):
            cols = slice(lo, lo + TILE)
            yield cols, jnp.dot(hid[...], wd[t, :, cols], preferred_element_type=jnp.float32)

    def sib_copy(p):
        return pltpu.make_async_remote_copy(
            sib_out.at[p], sib_in.at[p], sb_s.at[p], sb_r.at[p],
            device_id=sibling, device_id_type=pl.DeviceIdType.MESH,
        )

    def ring_copy(way, k, h):
        return pltpu.make_async_remote_copy(
            ring_out.at[way, k, pl.ds(h * hr, hr)], ring_in.at[way, k, pl.ds(h * hr, hr)],
            rs_s.at[way, k, h], rs_r.at[way, k, h],
            device_id=toward[way], device_id_type=pl.DeviceIdType.MESH,
        )

    def to_sibling(t, p):
        down_copy(t).wait()
        for cols, tile in down_tiles(t):
            sib_out[p, :, cols] = tile.astype(jnp.bfloat16)
        sib_copy(p).start()

    def to_own(t, side):
        down_copy(t).wait()
        for cols, tile in down_tiles(t):
            own[side, :, cols] = tile

    def ring_send(way, k, h, p, side, chained):
        at_rows = pl.ds(h * hr, hr)
        value = own[side, at_rows, :] + sib_in[p, at_rows, :].astype(jnp.float32)
        if chained:
            ring_copy(way, k + 1, h).wait_recv()
            value = value + ring_in[way, k + 1, at_rows, :].astype(jnp.float32)
        ring_out[way, k, at_rows, :] = value.astype(jnp.bfloat16)
        ring_copy(way, k, h).start()

    to_sibling(0, 0)
    to_own(1, 0)
    sib_copy(0).wait_recv()
    ring_send(0, half, 0, 0, 0, False)
    ring_send(1, half, 1, 0, 0, False)

    def distance(it, c):
        k = half - 1 - it
        t = 2 + 4 * it

        def give(side, c):
            to_sibling(t + side, 1 + 2 * it + side)
            return c

        def keep(side, c):
            to_own(t + 2 + side, side)
            return c

        lax.fori_loop(0, 2, give, 0)
        lax.fori_loop(0, 2, keep, 0)
        for side in (0, 1):
            sib_copy(1 + 2 * it + side).wait_recv()
        for way in (0, 1):
            h = 1 - way

            @pl.when(k == half - 1)
            def _():
                ring_send(way, k, h, 1 + 2 * it + way, way, False)

            @pl.when(k < half - 1)
            def _():
                ring_send(way, k, h, 1 + 2 * it + way, way, True)

        for way in (0, 1):
            ring_send(way, k, way, 1 + 2 * it + way, way, True)
        return c

    lax.fori_loop(0, half - 1, distance, 0)
    last = 2 * half - 1
    to_sibling(n - 2, last)
    to_own(n - 1, 0)
    sib_copy(last).wait_recv()
    own[0] = own[0] + sib_in[last].astype(jnp.float32)
    for h_first in (1, 0):
        for way in (0, 1):
            h = h_first if way == 0 else 1 - h_first
            at_rows = pl.ds(h * hr, hr)
            ring_copy(way, 1, h).wait_recv()
            own[0, at_rows, :] = own[0, at_rows, :] + ring_in[way, 1, at_rows, :].astype(jnp.float32)
    o_ref[...] = own[0].astype(o_ref.dtype)

    def told(k, c):
        msg_copy(k, me).wait_send()
        return c

    lax.fori_loop(1, n, told, 0)
    own_across(me).wait_send()
    for way in (0, 1):
        for k in range(1, half + 1):
            for h in (0, 1):
                if k == half and h != way:
                    continue
                gather_copy(way, k, h, at(pos + sign[way] * (k - 1), core)).wait_send()
                across_copy(way, k, h, at(pos + sign[way] * k, core)).wait_send()
                ring_copy(way, k, h).wait_send()
    for p in range(2 * half):
        sib_copy(p).wait_send()


def ringed(n, tokens, norm_gain, gate_weight, up_weight, down_weight):
    rows, block = tokens.shape
    width = gate_weight.shape[1]
    half = n // 4
    bf16, f32 = jnp.bfloat16, jnp.float32
    dma = pltpu.SemaphoreType.DMA
    vmem = pl.BlockSpec(memory_space=pltpu.VMEM)
    hbm = pl.BlockSpec(memory_space=pl.ANY)
    return pl.pallas_call(
        functools.partial(ffn_kernel, n),
        out_shape=jax.ShapeDtypeStruct((rows, block), bf16),
        in_specs=[vmem, vmem, hbm, hbm, hbm],
        out_specs=vmem,
        scratch_shapes=[
            pltpu.VMEM((n, 2, rows, block // 2), bf16),
            pltpu.VMEM((NBUF, width, block), bf16),
            pltpu.VMEM((NBUF, width, block), bf16),
            pltpu.VMEM((n, width, block), bf16),
            pltpu.VMEM((width, rows), f32),
            pltpu.VMEM((width, rows), f32),
            pltpu.VMEM((rows, block), bf16),
            pltpu.VMEM((rows, width), bf16),
            pltpu.VMEM((rows, 128), f32),
            pltpu.VMEM((n, 1, block + 128), f32),
            pltpu.VMEM((2, rows, block), f32),
            pltpu.VMEM((2 * half, rows, block), bf16),
            pltpu.VMEM((2 * half, rows, block), bf16),
            pltpu.VMEM((2, half + 1, rows, block), bf16),
            pltpu.VMEM((2, half + 1, rows, block), bf16),
            dma((n,)), dma((n,)),
            dma((2, half + 1, 2)), dma((2, half + 1, 2)),
            dma((2, half + 1, 2)), dma((2, half + 1, 2)),
            dma, dma,
            dma((2, 2, NBUF)), dma((n,)),
            dma((2, half + 1, 2)), dma((2, half + 1, 2)),
            dma((2 * half,)), dma((2 * half,)),
        ],
        compiler_params=pltpu.CompilerParams(
            collective_id=0, has_side_effects=True, vmem_limit_bytes=64 * 2**20 - 2**17
        ),
        cost_estimate=pl.CostEstimate(
            flops=6 * rows * n * block * width, bytes_accessed=6 * n * block * width, transcendentals=rows * width
        ),
        name="ffn_ring",
    )(tokens, norm_gain, gate_weight.T, up_weight.T, down_weight)


def solution(mesh):
    n = mesh.shape["din"]

    def local(tokens, norm_gain, gate_weight, up_weight, down_weight):
        args = (tokens, norm_gain, gate_weight, up_weight, down_weight)
        if n == 16 and tokens.shape[0] == 128 and tokens.shape[1] % TILE == 0 and gate_weight.shape[1] % 16 == 0:
            return ringed(n, *args)
        return gathered(*args)

    in_specs = (P("grp", "din"), P("din"), P(None, "din"), P(None, "din"), P("din", None))
    out_specs = P("grp", "din")
    return jax.shard_map(local, mesh=mesh, in_specs=in_specs, out_specs=out_specs, check_vma=False)
```

```python
import functools

import jax
import jax.numpy as jnp
from jax import lax
from jax.experimental import pallas as pl
from jax.experimental.pallas import tpu as pltpu
from jax.sharding import PartitionSpec as P

NBUF = 4
EARLY = 4
TILE = 256
EPS = 1e-05


def gathered(tokens, norm_gain, gate_weight, up_weight, down_weight):
    whole, gain = (
        lax.all_gather(tokens, "din", axis=1, tiled=True),
        lax.all_gather(norm_gain, "din", axis=0, tiled=True),
    )
    values = whole.astype(jnp.float32)
    inverse_rms = lax.rsqrt(jnp.mean(values * values, axis=1, keepdims=True) + EPS)
    normed = (values * gain.astype(jnp.float32) * inverse_rms).astype(jnp.bfloat16)
    gate = jnp.dot(normed, gate_weight, preferred_element_type=jnp.float32)
    up = jnp.dot(normed, up_weight, preferred_element_type=jnp.float32)
    hidden = (jax.nn.silu(gate) * up).astype(jnp.bfloat16)
    partial_terms = jnp.dot(hidden, down_weight, preferred_element_type=jnp.float32)
    return lax.psum_scatter(partial_terms, "din", scatter_dimension=1, tiled=True).astype(
        jnp.bfloat16
    )


def across_last(a, b):
    return lax.dot_general(a, b, (((1,), (1,)), ((), ())), preferred_element_type=jnp.float32)


def ffn_kernel(
    n, x_ref, g_ref, wg_hbm, wu_hbm, wd_hbm, o_ref,
    xbuf, wg, wu, wd, acc_g, acc_u, normed, hid, inv, msg, own, sib_out, sib_in, ring_out, ring_in,
    msg_s, msg_r, ag_s, ag_r, xs_s, xs_r, xo_s, xo_r, w_sem, d_sem, rs_s, rs_r, sb_s, sb_r,
):
    chips = n // 2
    zs = chips // 2
    half = chips // 2
    rows, block = x_ref.shape
    hr = rows // 2
    hb = block // 2
    width = wg_hbm.shape[0]
    features = n * block
    me = lax.axis_index("din")
    core = me % 2
    my_z, my_y = me // 4, (me // 2) % 2
    pos = my_z + my_y * (chips - 1 - 2 * my_z)

    def at(p, c):
        p = (p + 2 * chips) % chips
        y = p // zs
        z = p + y * (chips - 1 - 2 * p)
        return (z * 2 + y) * 2 + c

    other = 1 - core
    sibling = {"din": at(pos, other)}
    toward = ({"din": at(pos + 1, core)}, {"din": at(pos - 1, core)})
    sign = (-1, 1)

    def piece_at(u, e):
        k = (u + 2) // 4
        second = ((u + 2) % 4) // 2
        slot = at(pos + (2 * e - 1) * k, core + (u % 2) * (1 - 2 * core))
        return slot, e + second * (1 - 2 * e)

    def weight_copies(u):
        b = u % NBUF
        copies = []
        for e in (0, 1):
            slot, h = piece_at(u, e)
            source = pl.ds(pl.multiple_of(slot * block + h * hb, hb), hb)
            for which, (whole, held) in enumerate(((wg_hbm, wg), (wu_hbm, wu))):
                copies.append(
                    pltpu.make_async_copy(
                        whole.at[:, source], held.at[b, :, pl.ds(e * hb, hb)], w_sem.at[which, e, b]
                    )
                )
        return copies

    def dest_at(t):
        u = t + 2
        k = half - u // 4
        w = u % 4
        mine = jnp.where(k == half, w - 2, jnp.where(k == 0, w % 2, w // 2))
        side = jnp.where(k == half, 1, 1 - 2 * (w % 2))
        c = other + mine * (1 - 2 * other)
        return at(pos + side * k, c)

    def down_copy(t):
        start = pl.multiple_of(dest_at(t) * block, block)
        return pltpu.make_async_copy(wd_hbm.at[:, pl.ds(start, block)], wd.at[t], d_sem.at[t])

    for i in range(NBUF):
        for copy in weight_copies(i):
            copy.start()
    for t in range(EARLY):
        down_copy(t).start()

    barrier = pltpu.get_barrier_semaphore()

    def greet(k, c):
        pl.semaphore_signal(barrier, inc=1, device_id={"din": (me + k) % n}, device_id_type=pl.DeviceIdType.MESH)
        return c

    lax.fori_loop(1, n, greet, 0)

    for h in (0, 1):
        xbuf[me, h] = x_ref[:, h * hb : (h + 1) * hb]
    values = x_ref[...].astype(jnp.float32)
    squares = jnp.sum(values * values, axis=1, keepdims=True)
    msg[me, :, :block] = g_ref[...].astype(jnp.float32).reshape(1, block)
    msg[me, :, block:] = jnp.transpose(jnp.broadcast_to(squares, (rows, 128)))[0:1, :]
    acc_g[...] = jnp.zeros_like(acc_g)
    acc_u[...] = jnp.zeros_like(acc_u)

    pl.semaphore_wait(barrier, n - 1)

    def msg_copy(k, slot):
        return pltpu.make_async_remote_copy(
            msg.at[slot], msg.at[slot], msg_s.at[k], msg_r.at[k],
            device_id={"din": (me + k) % n}, device_id_type=pl.DeviceIdType.MESH,
        )

    def gather_copy(way, k, h, slot):
        part = xbuf.at[slot, h]
        return pltpu.make_async_remote_copy(
            part, part, ag_s.at[way, k, h], ag_r.at[way, k, h],
            device_id=toward[way], device_id_type=pl.DeviceIdType.MESH,
        )

    def across_copy(way, k, h, slot):
        part = xbuf.at[slot, h]
        return pltpu.make_async_remote_copy(
            part, part, xs_s.at[way, k, h], xs_r.at[way, k, h],
            device_id=sibling, device_id_type=pl.DeviceIdType.MESH,
        )

    def own_across(slot):
        return pltpu.make_async_remote_copy(
            xbuf.at[slot], xbuf.at[slot], xo_s, xo_r,
            device_id=sibling, device_id_type=pl.DeviceIdType.MESH,
        )

    def tell(k, c):
        msg_copy(k, me).start()
        return c

    for way in (0, 1):
        gather_copy(way, 1, way, me).start()
    lax.fori_loop(1, n, tell, 0)
    for way in (0, 1):
        gather_copy(way, 1, 1 - way, me).start()
    own_across(me).start()

    def hear(k, c):
        msg_copy(k, (me - k + n) % n).wait_recv()
        return c

    lax.fori_loop(1, n, hear, 0)
    total = msg[0, :, block:]
    for i in range(1, n):
        total = total + msg[i, :, block:]
    scale = lax.rsqrt(total / features + EPS)
    inv[...] = jnp.transpose(jnp.broadcast_to(scale, (128, rows)))

    def pass_on(k, second):
        for way in (0, 1):
            h = way if not second else 1 - way
            slot = at(pos + sign[way] * k, core)
            gather_copy(way, k, h, slot).wait_recv()

            if second:
                @pl.when(k < half - 1)
                def _():
                    gather_copy(way, k + 1, h, slot).start()
            else:
                @pl.when(k < half)
                def _():
                    gather_copy(way, k + 1, h, slot).start()
            across_copy(way, k, h, slot).start()

    def across_wait(k, second):
        for way in (0, 1):
            h = way if not second else 1 - way
            across_copy(way, k, h, at(pos + sign[way] * k, other)).wait_recv()

    def unit(u, c):
        k = (u + 2) // 4
        second = ((u + 2) % 4) // 2
        piece = jnp.where(u == n - 2, n // 2 - 1, jnp.where(u > n - 4, 0, (u + 1) // 2))
        due = jnp.where(u == n - 2, 1, u % 2) * jnp.minimum(piece, 1)

        @pl.when(u == 1)
        def _():
            own_across(at(pos, other)).wait_recv()

        for turn in (0, 1):
            @pl.when(jnp.logical_and(due == 1, (piece + 1) % 2 == turn))
            def _():
                pass_on((piece + 1) // 2, turn == 1)

            @pl.when(jnp.logical_and(jnp.logical_and(u > 1, second == turn), u % 2 == 1))
            def _():
                across_wait(k, turn == 1)

        for e in (0, 1):
            slot, h = piece_at(u, e)
            gain = msg[slot, :, pl.ds(pl.multiple_of(h * hb, hb), hb)]
            normed[:, e * hb : (e + 1) * hb] = (
                xbuf[slot, h].astype(jnp.float32) * gain * inv[:, 0:1]
            ).astype(jnp.bfloat16)
        for copy in weight_copies(u):
            copy.wait()
        b = u % NBUF
        acc_g[...] += across_last(wg[b], normed[...])
        acc_u[...] += across_last(wu[b], normed[...])

        @pl.when(u + NBUF < n)
        def _():
            for copy in weight_copies(u + NBUF):
                copy.start()

        @pl.when(u + EARLY < n)
        def _():
            down_copy(u + EARLY).start()

        return c

    lax.fori_loop(0, n, unit, 0)

    for lo in range(0, width, 128):
        part = slice(lo, min(lo + 128, width))
        gate = acc_g[part]
        hidden = gate / (1.0 + jnp.exp(-gate)) * acc_u[part]
        hid[:, part] = jnp.transpose(hidden).astype(jnp.bfloat16)

    def down_tiles(t):
        for lo in range(0, block, TILE):
            cols = slice(lo, lo + TILE)
            yield cols, jnp.dot(hid[...], wd[t, :, cols], preferred_element_type=jnp.float32)

    def sib_copy(p):
        return pltpu.make_async_remote_copy(
            sib_out.at[p], sib_in.at[p], sb_s.at[p], sb_r.at[p],
            device_id=sibling, device_id_type=pl.DeviceIdType.MESH,
        )

    def ring_copy(way, k, h):
        return pltpu.make_async_remote_copy(
            ring_out.at[way, k, pl.ds(h * hr, hr)], ring_in.at[way, k, pl.ds(h * hr, hr)],
            rs_s.at[way, k, h], rs_r.at[way, k, h],
            device_id=toward[way], device_id_type=pl.DeviceIdType.MESH,
        )

    def to_sibling(t, p):
        down_copy(t).wait()
        for cols, tile in down_tiles(t):
            sib_out[p, :, cols] = tile.astype(jnp.bfloat16)
        sib_copy(p).start()

    def to_own(t, side):
        down_copy(t).wait()
        for cols, tile in down_tiles(t):
            own[side, :, cols] = tile

    def ring_send(way, k, h, p, side, chained):
        at_rows = pl.ds(h * hr, hr)
        value = own[side, at_rows, :] + sib_in[p, at_rows, :].astype(jnp.float32)
        if chained:
            ring_copy(way, k + 1, h).wait_recv()
            value = value + ring_in[way, k + 1, at_rows, :].astype(jnp.float32)
        ring_out[way, k, at_rows, :] = value.astype(jnp.bfloat16)
        ring_copy(way, k, h).start()

    to_sibling(0, 0)
    to_own(1, 0)
    sib_copy(0).wait_recv()
    ring_send(0, half, 0, 0, 0, False)
    ring_send(1, half, 1, 0, 0, False)

    def distance(it, c):
        k = half - 1 - it
        t = 2 + 4 * it

        def give(side, c):
            to_sibling(t + side, 1 + 2 * it + side)
            return c

        def keep(side, c):
            to_own(t + 2 + side, side)
            return c

        lax.fori_loop(0, 2, give, 0)
        lax.fori_loop(0, 2, keep, 0)
        for side in (0, 1):
            sib_copy(1 + 2 * it + side).wait_recv()
        for way in (0, 1):
            h = 1 - way

            @pl.when(k == half - 1)
            def _():
                ring_send(way, k, h, 1 + 2 * it + way, way, False)

            @pl.when(k < half - 1)
            def _():
                ring_send(way, k, h, 1 + 2 * it + way, way, True)

        for way in (0, 1):
            ring_send(way, k, way, 1 + 2 * it + way, way, True)
        return c

    lax.fori_loop(0, half - 1, distance, 0)
    last = 2 * half - 1
    to_sibling(n - 2, last)
    to_own(n - 1, 0)
    sib_copy(last).wait_recv()
    own[0] = own[0] + sib_in[last].astype(jnp.float32)
    for h_first in (1, 0):
        for way in (0, 1):
            h = h_first if way == 0 else 1 - h_first
            at_rows = pl.ds(h * hr, hr)
            ring_copy(way, 1, h).wait_recv()
            own[0, at_rows, :] = own[0, at_rows, :] + ring_in[way, 1, at_rows, :].astype(jnp.float32)
    o_ref[...] = own[0].astype(o_ref.dtype)

    def told(k, c):
        msg_copy(k, me).wait_send()
        return c

    lax.fori_loop(1, n, told, 0)
    own_across(me).wait_send()
    for way in (0, 1):
        for k in range(1, half + 1):
            for h in (0, 1):
                if k == half and h != way:
                    continue
                gather_copy(way, k, h, at(pos + sign[way] * (k - 1), core)).wait_send()
                across_copy(way, k, h, at(pos + sign[way] * k, core)).wait_send()
                ring_copy(way, k, h).wait_send()
    for p in range(2 * half):
        sib_copy(p).wait_send()


def ringed(n, tokens, norm_gain, gate_weight, up_weight, down_weight):
    rows, block = tokens.shape
    width = gate_weight.shape[1]
    half = n // 4
    bf16, f32 = jnp.bfloat16, jnp.float32
    dma = pltpu.SemaphoreType.DMA
    vmem = pl.BlockSpec(memory_space=pltpu.VMEM)
    hbm = pl.BlockSpec(memory_space=pl.ANY)
    return pl.pallas_call(
        functools.partial(ffn_kernel, n),
        out_shape=jax.ShapeDtypeStruct((rows, block), bf16),
        in_specs=[vmem, vmem, hbm, hbm, hbm],
        out_specs=vmem,
        scratch_shapes=[
            pltpu.VMEM((n, 2, rows, block // 2), bf16),
            pltpu.VMEM((NBUF, width, block), bf16),
            pltpu.VMEM((NBUF, width, block), bf16),
            pltpu.VMEM((n, width, block), bf16),
            pltpu.VMEM((width, rows), f32),
            pltpu.VMEM((width, rows), f32),
            pltpu.VMEM((rows, block), bf16),
            pltpu.VMEM((rows, width), bf16),
            pltpu.VMEM((rows, 128), f32),
            pltpu.VMEM((n, 1, block + 128), f32),
            pltpu.VMEM((2, rows, block), f32),
            pltpu.VMEM((2 * half, rows, block), bf16),
            pltpu.VMEM((2 * half, rows, block), bf16),
            pltpu.VMEM((2, half + 1, rows, block), bf16),
            pltpu.VMEM((2, half + 1, rows, block), bf16),
            dma((n,)), dma((n,)),
            dma((2, half + 1, 2)), dma((2, half + 1, 2)),
            dma((2, half + 1, 2)), dma((2, half + 1, 2)),
            dma, dma,
            dma((2, 2, NBUF)), dma((n,)),
            dma((2, half + 1, 2)), dma((2, half + 1, 2)),
            dma((2 * half,)), dma((2 * half,)),
        ],
        compiler_params=pltpu.CompilerParams(
            collective_id=0, has_side_effects=True, vmem_limit_bytes=64 * 2**20 - 2**17
        ),
        cost_estimate=pl.CostEstimate(
            flops=6 * rows * n * block * width, bytes_accessed=6 * n * block * width, transcendentals=rows * width
        ),
        name="ffn_ring",
    )(tokens, norm_gain, gate_weight.T, up_weight.T, down_weight)


def solution(mesh):
    n = mesh.shape["din"]

    def local(tokens, norm_gain, gate_weight, up_weight, down_weight):
        args = (tokens, norm_gain, gate_weight, up_weight, down_weight)
        if n == 16 and tokens.shape[0] == 128 and tokens.shape[1] % TILE == 0 and gate_weight.shape[1] % 16 == 0:
            return ringed(n, *args)
        return gathered(*args)

    in_specs = (P("grp", "din"), P("din"), P(None, "din"), P(None, "din"), P("din", None))
    out_specs = P("grp", "din")
    return jax.shard_map(local, mesh=mesh, in_specs=in_specs, out_specs=out_specs, check_vma=False)
```
